32 devices in a mesh: grp: 2 (over x), occ: 16 (over z, y, core).
Axes of the slice: x: 2, y: 2, z: 4, core: 2. Of those that a mesh axis runs over, the one named last changes fastest.
Arguments:
- tile_blocks: bfloat16 [128, 16, 128, 128], P(('grp', 'occ')), parts along dimension 0, may hold values from -0.1875 to 0.1875
- occupied_coeffs: bfloat16 [1536, 1024], P(('grp', 'occ')), parts along dimension 0, may hold values from -6 to 6
- tile_slot: int32 [128, 16], P(('grp', 'occ')), parts along dimension 0, may hold values from 0 to 3
- tile_column: int32 [128, 16], P(('grp', 'occ')), parts along dimension 0, may hold values from 0 to 7
- tile_count: int32 [128], P(('grp', 'occ')), parts along dimension 0, may hold values from 1 to 16, as said below
- row_blocks: int32 [128, 4], P('grp'), parts along dimension 0, may hold values from 0 to 7, as said below
- owner_map: int32 [32], P('grp'), parts along dimension 0, may hold values from 0 to 15, each once
Outputs:
- exchange_block: float32 [2048, 1024], P(('grp', 'occ')), parts along dimension 0
The draws below stay inside these ranges and needn't reach their ends.
There are 2 independent parts, one for each index of `grp`. The reference program is written for one: setup_inputs(seed, part) draws one part's arguments, and reference() takes and returns one part's arrays. A program takes and returns all parts, laid end to end along the dimension named above; each array names one. Nothing has to cross between parts.
Inputs may be any that keep to these rules, and one draw needn't show every extreme that they name: `row_blocks`: each row names 4 different basis blocks. `tile_count`: slots at or past the count are padding; some auxiliary function has exactly 16 live tiles in every draw.
All inputs are finite; a program needn't handle non-finite values.
Results may differ from the reference program's by a relative error of at most 0.00091.
Values may be sent and summed in bfloat16 or wider, within the bound.
A program may use at most 64 MiB of HBM per device.

```python
import math
import jax
import jax.numpy as jnp
from jax import lax

TILE = 128
NB = 8
NL = 1024
NOCC = 768
RMAX = 4
TMAX = 16
NAUX = 64
N_OCC = 16


def draw_row_blocks(key, part):
    key = jax.random.fold_in(key, 11)
    subkeys = jax.random.split(key, NAUX)
    picked = jax.vmap(lambda subkey: jax.random.permutation(subkey, NB)[:RMAX])(subkeys)
    return picked.astype(jnp.int32)


def draw_tile_count(key, part):
    key = jax.random.fold_in(key, 23)
    counts = jax.random.randint(key, (NAUX,), 1, TMAX + 1)
    position = jax.random.randint(jax.random.fold_in(key, 5), (), 0, NAUX)
    return counts.at[position].set(TMAX).astype(jnp.int32)


def set_ends(entries, stream_key, low, top_value):
    place = [jax.random.randint(jax.random.fold_in(stream_key, axis), (), 0, length) for axis, length in enumerate(entries.shape)]
    main_axis = entries.shape.index(max(entries.shape))
    next_to = place[:main_axis] + [(place[main_axis] + 1) % entries.shape[main_axis]] + place[main_axis + 1:]
    return entries.at[tuple(place)].set(low).at[tuple(next_to)].set(top_value)


def steps_of(rng, shape, pieces, least, high):
    gain = 1.0
    for dim, parts in pieces:
        draws = jax.random.uniform(jax.random.fold_in(jax.random.fold_in(rng, 6), dim), (parts,), jnp.float32, least / len(pieces), high / len(pieces))
        gain = gain * jnp.repeat(jnp.exp(draws), shape[dim] // parts).reshape((-1,) + (1,) * (len(shape) - 1 - dim))
    return gain


def gaussian(stream_key, extent, width, limit, shards=(), dtype=jnp.bfloat16):
    drawn = jax.random.normal(stream_key, extent, jnp.float32) * width
    if len(shards) > 0:
        drawn = steps_of(stream_key, extent, shards, -0.22, 0.18) * drawn
    return jnp.clip(drawn, min=-limit, max=limit).astype(dtype)


def setup_inputs(seed: int = 0, part: int = 0) -> dict:
    splits = jax.random.split(jax.random.key(seed), 8)
    part_splits = jax.random.split(jax.random.fold_in(splits[7], part), 8)
    return {
        "tile_blocks": gaussian(part_splits[0], (NAUX, TMAX, TILE, TILE), (TILE * TMAX // 2) ** -0.5, 0.1875, ((0, 16),)),
        "occupied_coeffs": gaussian(part_splits[1], (NOCC, NL), 1.0, 6.0, ((0, 16),)),
        "tile_slot": set_ends(jax.random.randint(part_splits[2], (NAUX, TMAX), 0, RMAX), jax.random.fold_in(part_splits[2], 1), 0, RMAX - 1).astype(jnp.int32),
        "tile_column": set_ends(jax.random.randint(part_splits[3], (NAUX, TMAX), 0, NB), jax.random.fold_in(part_splits[3], 1), 0, NB - 1).astype(jnp.int32),
        "tile_count": draw_tile_count(jax.random.fold_in(jax.random.fold_in(splits[7], part), 71), part),
        "row_blocks": draw_row_blocks(jax.random.fold_in(jax.random.fold_in(splits[7], part), 71), part),
        "owner_map": jax.random.permutation(part_splits[6], N_OCC).astype(jnp.int32),
    }


def half_block(tile_set, slot_row, column_row, number, coeff_blocks):
    gathered = jnp.take(coeff_blocks, column_row, axis=1).astype(jnp.float32)
    products = jnp.einsum('itn,tmn->itm', gathered, tile_set.astype(jnp.float32))
    active = jnp.arange(TMAX) < number
    weights = ((slot_row[:, None] == jnp.arange(RMAX)[None, :]) & active[:, None]).astype(jnp.float32)
    transformed = jnp.einsum('tr,itm->irm', weights, products, precision=lax.Precision.HIGHEST)
    return transformed.astype(jnp.bfloat16)

def reference(tile_blocks, occupied_coeffs, tile_slot, tile_column, tile_count, row_blocks, owner_map):
    coeff_blocks = occupied_coeffs.reshape(NOCC, NB, TILE)

    def accumulate(accumulated, members):
        tile_set, slot_row, column_row, number, rows_row = members
        transformed = half_block(tile_set, slot_row, column_row, number, coeff_blocks).astype(jnp.float32)
        outer_sum = jnp.einsum('irm,isn->rmsn', transformed, transformed, precision=lax.Precision.HIGHEST)
        placed = (rows_row[:, None] == jnp.arange(NB)[None, :]).astype(jnp.float32)
        shifted = jnp.einsum('rb,rmsn->bmsn', placed, outer_sum, precision=lax.Precision.HIGHEST)
        shifted = jnp.einsum('bmsn,sc->bmcn', shifted, placed, precision=lax.Precision.HIGHEST)
        return (accumulated + shifted, None)
    accumulated, unused = lax.scan(accumulate, jnp.zeros((NB, TILE, NB, TILE), jnp.float32), (tile_blocks, tile_slot, tile_column, tile_count, row_blocks))
    factor = 1.0 / math.sqrt(NAUX * NOCC)
    complete = accumulated.reshape(NL, NL) * factor
    grouped = complete.reshape(N_OCC, NL // N_OCC, NL)
    return jnp.take(grouped, owner_map, axis=0).reshape(NL, NL)
```

```python
import functools
import math

import jax
import jax.numpy as jnp
from jax import lax
from jax.experimental import pallas as pl
from jax.experimental.pallas import tpu as pltpu
from jax.sharding import PartitionSpec as P

MESH = pl.DeviceIdType.MESH
LIMIT = 48 * 1024 * 1024


def place(n):
    me = lax.axis_index("occ")
    return me, me // 4, (me // 2) % 2, me % 2


def index(z, y, c):
    return z * 4 + y * 2 + c


def greet(n, z, y, c):
    zs = n // 4
    grp = lax.axis_index("grp")
    others = [index((z + k) % zs, y, c) for k in range(1, zs)]
    others += [index(z, 1 - y, c), index(z, y, 1 - c)]
    barrier = pltpu.get_barrier_semaphore()
    for other in others:
        pl.semaphore_signal(barrier, inc=1, device_id=(grp, other), device_id_type=MESH)
    pl.semaphore_wait(barrier, len(others))


def gather_kernel(n, x_ref, o_ref, own_sem, sz, sy, sc, recv):
    zs = n // 4
    me, z, y, c = place(n)
    grp = lax.axis_index("grp")
    greet(n, z, y, c)

    def copy(src, slot, target, send):
        return pltpu.make_async_remote_copy(
            src_ref=src,
            dst_ref=o_ref.at[slot],
            send_sem=send,
            recv_sem=recv.at[slot],
            device_id=(grp, target),
            device_id_type=MESH,
        )

    def arrived(slot):
        copy(o_ref.at[slot], slot, index(z, y, 1 - c), sz.at[0]).wait_recv()

    sent = []

    def send(src, slot, target, sem):
        d = copy(src, slot, target, sem)
        d.start()
        sent.append(d)

    own = pltpu.make_async_copy(x_ref, o_ref.at[me], own_sem)
    own.start()
    for k in range(1, zs):
        send(x_ref, me, index((z + k) % zs, y, c), sz.at[k])
    send(x_ref, me, index(z, 1 - y, c), sy.at[0])
    send(x_ref, me, index(z, y, 1 - c), sc.at[0])
    for k in range(1, zs):
        slot = index((z + zs - k) % zs, y, c)
        arrived(slot)
        send(o_ref.at[slot], slot, index(z, 1 - y, c), sy.at[k])
        send(o_ref.at[slot], slot, index(z, y, 1 - c), sc.at[k])
    for k in range(zs):
        slot = index((z + zs - k) % zs, 1 - y, c)
        arrived(slot)
        send(o_ref.at[slot], slot, index(z, y, 1 - c), sc.at[zs + k])
    for k in range(zs):
        arrived(index((z + zs - k) % zs, y, 1 - c))
        arrived(index((z + zs - k) % zs, 1 - y, 1 - c))
    own.wait()
    for d in sent:
        d.wait_send()


def gather(n, x):
    zs = n // 4
    return pl.pallas_call(
        functools.partial(gather_kernel, n),
        out_shape=jax.ShapeDtypeStruct((n,) + x.shape, x.dtype),
        in_specs=[pl.BlockSpec(memory_space=pl.ANY)],
        out_specs=pl.BlockSpec(memory_space=pl.ANY),
        scratch_shapes=[
            pltpu.SemaphoreType.DMA,
            pltpu.SemaphoreType.DMA((zs,)),
            pltpu.SemaphoreType.DMA((zs,)),
            pltpu.SemaphoreType.DMA((2 * zs,)),
            pltpu.SemaphoreType.DMA((n,)),
        ],
        compiler_params=pltpu.CompilerParams(collective_id=0, has_side_effects=True),
        name="gather_coeffs",
    )(x)


def exchange_kernel(
    factor, tile_ref, c_ref, slot_ref, col_ref, count_ref, rows_ref, owner_ref, o_ref, acc, half, total
):
    aux, _, size, _ = tile_ref.shape
    slots = rows_ref.shape[1]
    groups, rows, _ = o_ref.shape
    total[...] = jnp.zeros_like(total)
    for p in range(aux):
        acc[...] = jnp.zeros_like(acc)

        def tile_step(t, carry):
            col = pl.ds(pl.multiple_of(col_ref[p, t] * size, size), size)
            dst = pl.ds(pl.multiple_of(slot_ref[p, t] * size, size), size)
            acc[:, dst] += lax.dot_general(
                c_ref[:, col],
                tile_ref[p, t],
                (((1,), (1,)), ((), ())),
                preferred_element_type=jnp.float32,
            )
            return carry

        lax.fori_loop(0, count_ref[p], tile_step, 0)
        half[...] = acc[...].astype(half.dtype)
        for r in range(slots):
            left = half[:, r * size : (r + 1) * size].T
            gram = jnp.dot(left, half[...], preferred_element_type=jnp.float32)
            row = pl.ds(pl.multiple_of(rows_ref[p, r] * size, size), size)
            for s in range(slots):
                column = pl.ds(pl.multiple_of(rows_ref[p, s] * size, size), size)
                total[row, column] += gram[:, s * size : (s + 1) * size]

    def emit(j, carry):
        src = pl.ds(pl.multiple_of(owner_ref[j] * rows, rows), rows)
        o_ref[j] = total[src, :] * factor
        return carry

    lax.fori_loop(0, groups, emit, 0)


def exchange(n, factor, tiles, coeffs, slot, column, count, rows, owner):
    aux, _, size, _ = tiles.shape
    occupied, region = coeffs.shape
    slots = rows.shape[1]
    vmem = pl.BlockSpec(memory_space=pltpu.VMEM)
    smem = pl.BlockSpec(memory_space=pltpu.SMEM)
    return pl.pallas_call(
        functools.partial(exchange_kernel, factor),
        out_shape=jax.ShapeDtypeStruct((n, region // n, region), jnp.float32),
        in_specs=[vmem, vmem, smem, smem, smem, smem, smem],
        out_specs=vmem,
        scratch_shapes=[
            pltpu.VMEM((occupied, slots * size), jnp.float32),
            pltpu.VMEM((occupied, slots * size), jnp.bfloat16),
            pltpu.VMEM((region, region), jnp.float32),
        ],
        compiler_params=pltpu.CompilerParams(vmem_limit_bytes=LIMIT),
        name="partial_exchange",
    )(tiles, coeffs, slot, column, count, rows, owner)


def local(tile_blocks, occupied_coeffs, tile_slot, tile_column, tile_count, row_blocks, owner_map):
    n = lax.axis_size("occ")
    aux_local = tile_blocks.shape[0]
    occupied = occupied_coeffs.shape[0] * n
    region = occupied_coeffs.shape[1]
    factor = 1.0 / math.sqrt(row_blocks.shape[0] * occupied)
    coeffs = gather(n, occupied_coeffs).reshape(occupied, region)
    own_rows = lax.dynamic_slice_in_dim(row_blocks, lax.axis_index("occ") * aux_local, aux_local, 0)
    partial = exchange(
        n, factor, tile_blocks, coeffs, tile_slot, tile_column, tile_count, own_rows, owner_map
    )
    return lax.psum_scatter(
        partial.reshape(region, region), "occ", scatter_dimension=0, tiled=True
    )


def solution(mesh):
    in_specs = (
        P(("grp", "occ"), None, None, None),
        P(("grp", "occ"), None),
        P(("grp", "occ"), None),
        P(("grp", "occ"), None),
        P(("grp", "occ")),
        P("grp", None),
        P("grp"),
    )
    out_specs = P(("grp", "occ"), None)
    return jax.shard_map(local, mesh=mesh, in_specs=in_specs, out_specs=out_specs, check_vma=False)
```

```python
import functools
import math

import jax
import jax.numpy as jnp
from jax import lax
from jax.experimental import pallas as pl
from jax.experimental.pallas import tpu as pltpu
from jax.sharding import PartitionSpec as P

MESH = pl.DeviceIdType.MESH
LIMIT = 48 * 1024 * 1024


def place(n):
    me = lax.axis_index("occ")
    return me, me // 4, (me // 2) % 2, me % 2


def index(z, y, c):
    return z * 4 + y * 2 + c


def greet(n, z, y, c):
    zs = n // 4
    grp = lax.axis_index("grp")
    others = [index((z + k) % zs, y, c) for k in range(1, zs)]
    others += [index(z, 1 - y, c), index(z, y, 1 - c)]
    barrier = pltpu.get_barrier_semaphore()
    for other in others:
        pl.semaphore_signal(barrier, inc=1, device_id=(grp, other), device_id_type=MESH)
    pl.semaphore_wait(barrier, len(others))


def gather_kernel(n, x_ref, o_ref, own_sem, sz, sy, sc, recv):
    zs = n // 4
    me, z, y, c = place(n)
    grp = lax.axis_index("grp")
    greet(n, z, y, c)

    def copy(src, slot, target, send):
        return pltpu.make_async_remote_copy(
            src_ref=src,
            dst_ref=o_ref.at[slot],
            send_sem=send,
            recv_sem=recv.at[slot],
            device_id=(grp, target),
            device_id_type=MESH,
        )

    def arrived(slot):
        copy(o_ref.at[slot], slot, index(z, y, 1 - c), sz.at[0]).wait_recv()

    sent = []

    def send(src, slot, target, sem):
        d = copy(src, slot, target, sem)
        d.start()
        sent.append(d)

    own = pltpu.make_async_copy(x_ref, o_ref.at[me], own_sem)
    own.start()
    for k in range(1, zs):
        send(x_ref, me, index((z + k) % zs, y, c), sz.at[k])
    send(x_ref, me, index(z, 1 - y, c), sy.at[0])
    send(x_ref, me, index(z, y, 1 - c), sc.at[0])
    for k in range(1, zs):
        slot = index((z + zs - k) % zs, y, c)
        arrived(slot)
        send(o_ref.at[slot], slot, index(z, 1 - y, c), sy.at[k])
        send(o_ref.at[slot], slot, index(z, y, 1 - c), sc.at[k])
    for k in range(zs):
        slot = index((z + zs - k) % zs, 1 - y, c)
        arrived(slot)
        send(o_ref.at[slot], slot, index(z, y, 1 - c), sc.at[zs + k])
    for k in range(zs):
        arrived(index((z + zs - k) % zs, y, 1 - c))
        arrived(index((z + zs - k) % zs, 1 - y, 1 - c))
    own.wait()
    for d in sent:
        d.wait_send()


def gather(n, x):
    zs = n // 4
    return pl.pallas_call(
        functools.partial(gather_kernel, n),
        out_shape=jax.ShapeDtypeStruct((n,) + x.shape, x.dtype),
        in_specs=[pl.BlockSpec(memory_space=pl.ANY)],
        out_specs=pl.BlockSpec(memory_space=pl.ANY),
        scratch_shapes=[
            pltpu.SemaphoreType.DMA,
            pltpu.SemaphoreType.DMA((zs,)),
            pltpu.SemaphoreType.DMA((zs,)),
            pltpu.SemaphoreType.DMA((2 * zs,)),
            pltpu.SemaphoreType.DMA((n,)),
        ],
        compiler_params=pltpu.CompilerParams(collective_id=0, has_side_effects=True),
        name="gather_coeffs",
    )(x)


def exchange_kernel(
    tile_hbm,
    c_hbm,
    slot_hbm,
    col_hbm,
    count_hbm,
    rows_hbm,
    owner_hbm,
    o_ref,
    tile_ref,
    c_ref,
    slot_ref,
    col_ref,
    count_ref,
    rows_ref,
    owner_ref,
    acc,
    half,
    total,
    in_sem,
    out_sem,
):
    aux, _, size, _ = tile_ref.shape
    slots = rows_ref.shape[1]
    groups, rows, _ = o_ref.shape
    pairs = (
        (slot_hbm, slot_ref),
        (col_hbm, col_ref),
        (count_hbm, count_ref),
        (rows_hbm, rows_ref),
        (owner_hbm, owner_ref),
        (c_hbm, c_ref),
        (tile_hbm, tile_ref),
    )
    loads = [pltpu.make_async_copy(src, dst, in_sem.at[k]) for k, (src, dst) in enumerate(pairs)]
    for load in loads:
        load.start()
    total[...] = jnp.zeros_like(total)
    acc[...] = jnp.zeros_like(acc)
    for load in loads:
        load.wait()
    for p in range(aux):
        if p:
            acc[...] = jnp.zeros_like(acc)

        def tile_step(t, carry):
            col = pl.ds(pl.multiple_of(col_ref[p, t] * size, size), size)
            dst = pl.ds(pl.multiple_of(slot_ref[p, t] * size, size), size)
            acc[:, dst] += lax.dot_general(
                c_ref[:, col],
                tile_ref[p, t],
                (((1,), (1,)), ((), ())),
                preferred_element_type=jnp.float32,
            )
            return carry

        lax.fori_loop(0, count_ref[p], tile_step, 0)
        half[...] = acc[...].astype(half.dtype)
        for r in range(slots):
            left = half[:, r * size : (r + 1) * size].T
            gram = jnp.dot(left, half[...], preferred_element_type=jnp.float32)
            row = pl.ds(pl.multiple_of(rows_ref[p, r] * size, size), size)
            for s in range(slots):
                column = pl.ds(pl.multiple_of(rows_ref[p, s] * size, size), size)
                total[row, column] += gram[:, s * size : (s + 1) * size]
    stores = []
    for j in range(groups):
        src = pl.ds(pl.multiple_of(owner_ref[j] * rows, rows), rows)
        stores.append(pltpu.make_async_copy(total.at[src], o_ref.at[j], out_sem.at[j]))
        stores[-1].start()
    for store in stores:
        store.wait()


def exchange(n, tiles, coeffs, slot, column, count, rows, owner):
    aux, _, size, _ = tiles.shape
    occupied, region = coeffs.shape
    slots = rows.shape[1]
    anywhere = pl.BlockSpec(memory_space=pl.ANY)
    return pl.pallas_call(
        exchange_kernel,
        out_shape=jax.ShapeDtypeStruct((n, region // n, region), jnp.float32),
        in_specs=[anywhere] * 7,
        out_specs=anywhere,
        scratch_shapes=[
            pltpu.VMEM(tiles.shape, tiles.dtype),
            pltpu.VMEM(coeffs.shape, coeffs.dtype),
            pltpu.SMEM(slot.shape, slot.dtype),
            pltpu.SMEM(column.shape, column.dtype),
            pltpu.SMEM(count.shape, count.dtype),
            pltpu.SMEM(rows.shape, rows.dtype),
            pltpu.SMEM(owner.shape, owner.dtype),
            pltpu.VMEM((occupied, slots * size), jnp.float32),
            pltpu.VMEM((occupied, slots * size), jnp.bfloat16),
            pltpu.VMEM((region, region), jnp.float32),
            pltpu.SemaphoreType.DMA((7,)),
            pltpu.SemaphoreType.DMA((n,)),
        ],
        compiler_params=pltpu.CompilerParams(vmem_limit_bytes=LIMIT),
        name="partial_exchange",
    )(tiles, coeffs, slot, column, count, rows, owner)


def scatter_kernel(
    n, factor, x_ref, o_ref, acc, in1, in2, in3, load_sem, s1, r1, s2, r2, s3, r3
):
    zs = n // 4
    me, z, y, c = place(n)
    grp = lax.axis_index("grp")
    greet(n, z, y, c)
    planes = [(z + k) % zs for k in [zs // 2 + (k + 1) // 2 * (1 - 2 * (k % 2)) for k in range(zs - 1)]]
    planes.append(z)

    def core_copy(zz, yy):
        k = zz * 2 + yy
        return pltpu.make_async_remote_copy(
            src_ref=x_ref.at[index(zz, yy, 1 - c)],
            dst_ref=in1.at[k],
            send_sem=s1.at[k],
            recv_sem=r1.at[k],
            device_id=(grp, index(z, y, 1 - c)),
            device_id_type=MESH,
        )

    def load(zz, yy):
        k = zz * 2 + yy
        return pltpu.make_async_copy(x_ref.at[index(zz, yy, c)], acc.at[k], load_sem.at[k])

    def y_copy(zz):
        return pltpu.make_async_remote_copy(
            src_ref=acc.at[zz * 2 + 1 - y],
            dst_ref=in2.at[zz],
            send_sem=s2.at[zz],
            recv_sem=r2.at[zz],
            device_id=(grp, index(z, 1 - y, c)),
            device_id_type=MESH,
        )

    def z_copy(zz, slot):
        return pltpu.make_async_remote_copy(
            src_ref=acc.at[zz * 2 + y],
            dst_ref=in3.at[slot],
            send_sem=s3.at[zz],
            recv_sem=r3.at[slot],
            device_id=(grp, index(zz, y, c)),
            device_id_type=MESH,
        )

    order = [(zz, yy) for yy in (1 - y, y) for zz in planes]
    for zz, yy in order:
        core_copy(zz, yy).start()
        load(zz, yy).start()
    for zz in planes:
        k = zz * 2 + 1 - y
        load(zz, 1 - y).wait()
        core_copy(zz, 1 - y).wait_recv()
        acc[k] = acc[k] + in1[k]
        y_copy(zz).start()
    for zz in planes[:-1]:
        k = zz * 2 + y
        load(zz, y).wait()
        core_copy(zz, y).wait_recv()
        y_copy(zz).wait_recv()
        acc[k] = acc[k] + in1[k] + in2[zz]
        z_copy(zz, z).start()
    k = z * 2 + y
    load(z, y).wait()
    core_copy(z, y).wait_recv()
    y_copy(z).wait_recv()
    acc[k] = acc[k] + in1[k] + in2[z]
    for zz in planes[:-1]:
        z_copy(zz, zz).wait_recv()
        acc[k] = acc[k] + in3[zz]
    o_ref[...] = acc[k] * factor
    for zz, yy in order:
        core_copy(zz, yy).wait_send()
    for zz in planes:
        y_copy(zz).wait_send()
    for zz in planes[:-1]:
        z_copy(zz, z).wait_send()


def scatter(n, factor, x):
    zs = n // 4
    block = x.shape[1:]
    dma = pltpu.SemaphoreType.DMA
    return pl.pallas_call(
        functools.partial(scatter_kernel, n, factor),
        out_shape=jax.ShapeDtypeStruct(block, x.dtype),
        in_specs=[pl.BlockSpec(memory_space=pl.ANY)],
        out_specs=pl.BlockSpec(memory_space=pltpu.VMEM),
        scratch_shapes=[
            pltpu.VMEM((n // 2,) + block, x.dtype),
            pltpu.VMEM((n // 2,) + block, x.dtype),
            pltpu.VMEM((zs,) + block, x.dtype),
            pltpu.VMEM((zs,) + block, x.dtype),
            dma((n // 2,)),
            dma((n // 2,)),
            dma((n // 2,)),
            dma((zs,)),
            dma((zs,)),
            dma((zs,)),
            dma((zs,)),
        ],
        compiler_params=pltpu.CompilerParams(
            collective_id=1, has_side_effects=True, vmem_limit_bytes=LIMIT
        ),
        name="scatter_exchange",
    )(x)


def local(tile_blocks, occupied_coeffs, tile_slot, tile_column, tile_count, row_blocks, owner_map):
    n = lax.axis_size("occ")
    aux_local = tile_blocks.shape[0]
    occupied = occupied_coeffs.shape[0] * n
    region = occupied_coeffs.shape[1]
    factor = 1.0 / math.sqrt(row_blocks.shape[0] * occupied)
    coeffs = gather(n, occupied_coeffs).reshape(occupied, region)
    own_rows = lax.dynamic_slice_in_dim(row_blocks, lax.axis_index("occ") * aux_local, aux_local, 0)
    partial = exchange(
        n, tile_blocks, coeffs, tile_slot, tile_column, tile_count, own_rows, owner_map
    )
    return scatter(n, factor, partial)


def solution(mesh):
    in_specs = (
        P(("grp", "occ"), None, None, None),
        P(("grp", "occ"), None),
        P(("grp", "occ"), None),
        P(("grp", "occ"), None),
        P(("grp", "occ")),
        P("grp", None),
        P("grp"),
    )
    out_specs = P(("grp", "occ"), None)
    return jax.shard_map(local, mesh=mesh, in_specs=in_specs, out_specs=out_specs, check_vma=False)
```

```python
import functools
import math

import jax
import jax.numpy as jnp
from jax import lax
from jax.experimental import pallas as pl
from jax.experimental.pallas import tpu as pltpu
from jax.sharding import PartitionSpec as P

MESH = pl.DeviceIdType.MESH
LIMIT = 60 * 1024 * 1024


def place(n):
    me = lax.axis_index("occ")
    return me, me // 4, (me // 2) % 2, me % 2


def index(z, y, c):
    return z * 4 + y * 2 + c


def greet(n, z, y, c):
    zs = n // 4
    grp = lax.axis_index("grp")
    others = [index((z + k) % zs, y, c) for k in range(1, zs)]
    others += [index(z, 1 - y, c), index(z, y, 1 - c)]
    barrier = pltpu.get_barrier_semaphore()
    for other in others:
        pl.semaphore_signal(barrier, inc=1, device_id=(grp, other), device_id_type=MESH)
    pl.semaphore_wait(barrier, len(others))


def gather_kernel(n, x_ref, o_ref, own_sem, s_up, s_down, s_y, s_c, recv):
    zs = n // 4
    me, z, y, c = place(n)
    grp = lax.axis_index("grp")
    greet(n, z, y, c)

    def copy(slot, target, send, own=False):
        return pltpu.make_async_remote_copy(
            src_ref=x_ref if own else o_ref.at[slot],
            dst_ref=o_ref.at[slot],
            send_sem=send,
            recv_sem=recv.at[slot],
            device_id=(grp, target),
            device_id_type=MESH,
        )

    def up(s):
        return copy(index(z - s, y, c), index(z + 1, y, c), s_up.at[s], s == 0)

    def down(s):
        return copy(index(z + s, y, c), index(z - 1, y, c), s_down.at[s], s == 0)

    def across(zz, own=False):
        return copy(index(zz, y, c), index(z, 1 - y, c), s_y.at[zz], own)

    def over(zz, yy, own=False):
        return copy(index(zz, yy, c), index(z, y, 1 - c), s_c.at[zz * 2 + yy], own)

    def pass_on(zz):
        over(zz, y).wait_recv()

    own = pltpu.make_async_copy(x_ref, o_ref.at[me], own_sem)
    own.start()
    for s in range(zs):
        below, above = z - s >= 0, z + s < zs
        if s:
            pl.when(below)(lambda: pass_on(z - s))
        if s < zs - 1:
            pl.when(below & (z + 1 < zs))(lambda: up(s).start())
        if s:
            pl.when(above)(lambda: pass_on(z + s))
        if s < zs - 1:
            pl.when(above & (z >= 1))(lambda: down(s).start())
        if s == 0:
            across(z, True).start()
            over(z, y, True).start()
        else:

            def forward(zz):
                across(zz).start()
                over(zz, y).start()

            pl.when(below)(lambda: forward(z - s))
            pl.when(above)(lambda: forward(z + s))
    reach = [0] + [d * s for s in range(1, zs) for d in (-1, 1)]

    def relay(zz):
        over(zz, 1 - y).wait_recv()
        over(zz, 1 - y).start()

    for d in reach:
        zz = z + d
        pl.when((zz >= 0) & (zz < zs))(lambda: relay(zz))
    for zz in range(zs):
        for yy in range(2):
            copy(index(zz, yy, 1 - c), index(z, y, 1 - c), s_c.at[0]).wait_recv()
    own.wait()
    for s in range(zs - 1):
        pl.when((z - s >= 0) & (z + 1 < zs))(lambda: up(s).wait_send())
        pl.when((z + s < zs) & (z >= 1))(lambda: down(s).wait_send())
    for zz in range(zs):
        across(zz).wait_send()
        for yy in range(2):
            over(zz, yy).wait_send()


def gather(n, x):
    zs = n // 4
    dma = pltpu.SemaphoreType.DMA
    return pl.pallas_call(
        functools.partial(gather_kernel, n),
        out_shape=jax.ShapeDtypeStruct((n,) + x.shape, x.dtype),
        in_specs=[pl.BlockSpec(memory_space=pl.ANY)],
        out_specs=pl.BlockSpec(memory_space=pl.ANY),
        scratch_shapes=[dma, dma((zs,)), dma((zs,)), dma((zs,)), dma((2 * zs,)), dma((n,))],
        compiler_params=pltpu.CompilerParams(
            collective_id=0, has_side_effects=True, vmem_limit_bytes=LIMIT
        ),
        name="gather_coeffs",
    )(x)


def exchange_kernel(
    tile_hbm,
    c_hbm,
    slot_hbm,
    col_hbm,
    count_hbm,
    rows_hbm,
    owner_hbm,
    o_ref,
    tile_ref,
    c_ref,
    slot_ref,
    col_ref,
    count_ref,
    rows_ref,
    owner_ref,
    acc,
    half,
    total,
    in_sem,
    out_sem,
):
    aux, _, size, _ = tile_ref.shape
    slots = rows_ref.shape[1]
    groups, rows, _ = o_ref.shape
    pairs = (
        (slot_hbm, slot_ref),
        (col_hbm, col_ref),
        (count_hbm, count_ref),
        (rows_hbm, rows_ref),
        (owner_hbm, owner_ref),
        (c_hbm, c_ref),
        (tile_hbm, tile_ref),
    )
    loads = [pltpu.make_async_copy(src, dst, in_sem.at[k]) for k, (src, dst) in enumerate(pairs)]
    for load in loads:
        load.start()
    total[...] = jnp.zeros_like(total)
    acc[...] = jnp.zeros_like(acc)
    for load in loads:
        load.wait()
    for p in range(aux):
        if p:
            acc[...] = jnp.zeros_like(acc)

        def tile_step(t, carry):
            col = pl.ds(pl.multiple_of(col_ref[p, t] * size, size), size)
            dst = pl.ds(pl.multiple_of(slot_ref[p, t] * size, size), size)
            acc[:, dst] += lax.dot_general(
                c_ref[:, col],
                tile_ref[p, t],
                (((1,), (1,)), ((), ())),
                preferred_element_type=jnp.float32,
            )
            return carry

        lax.fori_loop(0, count_ref[p], tile_step, 0)
        half[...] = acc[...].astype(half.dtype)
        for r in range(slots):
            left = half[:, r * size : (r + 1) * size].T
            gram = jnp.dot(left, half[...], preferred_element_type=jnp.float32)
            row = pl.ds(pl.multiple_of(rows_ref[p, r] * size, size), size)
            for s in range(slots):
                column = pl.ds(pl.multiple_of(rows_ref[p, s] * size, size), size)
                total[row, column] += gram[:, s * size : (s + 1) * size]
    stores = []
    for j in range(groups):
        src = pl.ds(pl.multiple_of(owner_ref[j] * rows, rows), rows)
        stores.append(pltpu.make_async_copy(total.at[src], o_ref.at[j], out_sem.at[j]))
        stores[-1].start()
    for store in stores:
        store.wait()


def exchange(n, tiles, coeffs, slot, column, count, rows, owner):
    aux, _, size, _ = tiles.shape
    occupied, region = coeffs.shape
    slots = rows.shape[1]
    anywhere = pl.BlockSpec(memory_space=pl.ANY)
    return pl.pallas_call(
        exchange_kernel,
        out_shape=jax.ShapeDtypeStruct((n, region // n, region), jnp.float32),
        in_specs=[anywhere] * 7,
        out_specs=anywhere,
        scratch_shapes=[
            pltpu.VMEM(tiles.shape, tiles.dtype),
            pltpu.VMEM(coeffs.shape, coeffs.dtype),
            pltpu.SMEM(slot.shape, slot.dtype),
            pltpu.SMEM(column.shape, column.dtype),
            pltpu.SMEM(count.shape, count.dtype),
            pltpu.SMEM(rows.shape, rows.dtype),
            pltpu.SMEM(owner.shape, owner.dtype),
            pltpu.VMEM((occupied, slots * size), jnp.float32),
            pltpu.VMEM((occupied, slots * size), jnp.bfloat16),
            pltpu.VMEM((region, region), jnp.float32),
            pltpu.SemaphoreType.DMA((7,)),
            pltpu.SemaphoreType.DMA((n,)),
        ],
        compiler_params=pltpu.CompilerParams(vmem_limit_bytes=LIMIT),
        name="partial_exchange",
    )(tiles, coeffs, slot, column, count, rows, owner)


def scatter_kernel(
    n, factor, x_ref, o_ref, acc, in1, in2, in3, load_sem, s1, r1, s2, r2, s3, r3
):
    zs = n // 4
    me, z, y, c = place(n)
    grp = lax.axis_index("grp")
    greet(n, z, y, c)
    planes = [(z + k) % zs for k in [zs // 2 + (k + 1) // 2 * (1 - 2 * (k % 2)) for k in range(zs - 1)]]
    planes.append(z)

    def core_copy(zz, yy):
        k = zz * 2 + yy
        return pltpu.make_async_remote_copy(
            src_ref=x_ref.at[index(zz, yy, 1 - c)],
            dst_ref=in1.at[k],
            send_sem=s1.at[k],
            recv_sem=r1.at[k],
            device_id=(grp, index(z, y, 1 - c)),
            device_id_type=MESH,
        )

    def load(zz, yy):
        k = zz * 2 + yy
        return pltpu.make_async_copy(x_ref.at[index(zz, yy, c)], acc.at[k], load_sem.at[k])

    def y_copy(zz):
        return pltpu.make_async_remote_copy(
            src_ref=acc.at[zz * 2 + 1 - y],
            dst_ref=in2.at[zz],
            send_sem=s2.at[zz],
            recv_sem=r2.at[zz],
            device_id=(grp, index(z, 1 - y, c)),
            device_id_type=MESH,
        )

    def z_copy(zz, slot):
        return pltpu.make_async_remote_copy(
            src_ref=acc.at[zz * 2 + y],
            dst_ref=in3.at[slot],
            send_sem=s3.at[zz],
            recv_sem=r3.at[slot],
            device_id=(grp, index(zz, y, c)),
            device_id_type=MESH,
        )

    order = [(zz, yy) for yy in (1 - y, y) for zz in planes]
    for zz, yy in order:
        core_copy(zz, yy).start()
        load(zz, yy).start()
    for zz in planes:
        k = zz * 2 + 1 - y
        load(zz, 1 - y).wait()
        core_copy(zz, 1 - y).wait_recv()
        acc[k] = acc[k] + in1[k]
        y_copy(zz).start()
    for zz in planes[:-1]:
        k = zz * 2 + y
        load(zz, y).wait()
        core_copy(zz, y).wait_recv()
        y_copy(zz).wait_recv()
        acc[k] = acc[k] + in1[k] + in2[zz]
        z_copy(zz, z).start()
    k = z * 2 + y
    load(z, y).wait()
    core_copy(z, y).wait_recv()
    y_copy(z).wait_recv()
    acc[k] = acc[k] + in1[k] + in2[z]
    for zz in planes[:-1]:
        z_copy(zz, zz).wait_recv()
        acc[k] = acc[k] + in3[zz]
    o_ref[...] = acc[k] * factor
    for zz, yy in order:
        core_copy(zz, yy).wait_send()
    for zz in planes:
        y_copy(zz).wait_send()
    for zz in planes[:-1]:
        z_copy(zz, z).wait_send()


def scatter(n, factor, x):
    zs = n // 4
    block = x.shape[1:]
    dma = pltpu.SemaphoreType.DMA
    return pl.pallas_call(
        functools.partial(scatter_kernel, n, factor),
        out_shape=jax.ShapeDtypeStruct(block, x.dtype),
        in_specs=[pl.BlockSpec(memory_space=pl.ANY)],
        out_specs=pl.BlockSpec(memory_space=pltpu.VMEM),
        scratch_shapes=[
            pltpu.VMEM((n // 2,) + block, x.dtype),
            pltpu.VMEM((n // 2,) + block, x.dtype),
            pltpu.VMEM((zs,) + block, x.dtype),
            pltpu.VMEM((zs,) + block, x.dtype),
            dma((n // 2,)),
            dma((n // 2,)),
            dma((n // 2,)),
            dma((zs,)),
            dma((zs,)),
            dma((zs,)),
            dma((zs,)),
        ],
        compiler_params=pltpu.CompilerParams(
            collective_id=1, has_side_effects=True, vmem_limit_bytes=LIMIT
        ),
        name="scatter_exchange",
    )(x)


def local(tile_blocks, occupied_coeffs, tile_slot, tile_column, tile_count, row_blocks, owner_map):
    n = lax.axis_size("occ")
    aux_local = tile_blocks.shape[0]
    occupied = occupied_coeffs.shape[0] * n
    region = occupied_coeffs.shape[1]
    factor = 1.0 / math.sqrt(row_blocks.shape[0] * occupied)
    coeffs = gather(n, occupied_coeffs).reshape(occupied, region)
    own_rows = lax.dynamic_slice_in_dim(row_blocks, lax.axis_index("occ") * aux_local, aux_local, 0)
    partial = exchange(
        n, tile_blocks, coeffs, tile_slot, tile_column, tile_count, own_rows, owner_map
    )
    return scatter(n, factor, partial)


def solution(mesh):
    in_specs = (
        P(("grp", "occ"), None, None, None),
        P(("grp", "occ"), None),
        P(("grp", "occ"), None),
        P(("grp", "occ"), None),
        P(("grp", "occ")),
        P("grp", None),
        P("grp"),
    )
    out_specs = P(("grp", "occ"), None)
    return jax.shard_map(local, mesh=mesh, in_specs=in_specs, out_specs=out_specs, check_vma=False)
```

```python
import functools
import math

import jax
import jax.numpy as jnp
from jax import lax
from jax.experimental import pallas as pl
from jax.experimental.pallas import tpu as pltpu
from jax.sharding import PartitionSpec as P

MESH = pl.DeviceIdType.MESH
LIMIT = 60 * 1024 * 1024


def place(n):
    me = lax.axis_index("occ")
    return me, me // 4, (me // 2) % 2, me % 2


def index(z, y, c):
    return z * 4 + y * 2 + c


def greet_all(n, me):
    grp = lax.axis_index("grp")
    barrier = pltpu.get_barrier_semaphore()
    for k in range(1, n):
        pl.semaphore_signal(
            barrier, inc=1, device_id=(grp, (me + k) % n), device_id_type=MESH
        )
    pl.semaphore_wait(barrier, n - 1)


def greet(n, z, y, c):
    zs = n // 4
    grp = lax.axis_index("grp")
    others = [index((z + k) % zs, y, c) for k in range(1, zs)]
    others += [index(z, 1 - y, c), index(z, y, 1 - c)]
    barrier = pltpu.get_barrier_semaphore()
    for other in others:
        pl.semaphore_signal(barrier, inc=1, device_id=(grp, other), device_id_type=MESH)
    pl.semaphore_wait(barrier, len(others))


def gather_kernel(n, x_ref, o_ref, own_sem, s_up, s_down, s_y, s_c, recv):
    zs = n // 4
    me, z, y, c = place(n)
    grp = lax.axis_index("grp")
    greet(n, z, y, c)

    def copy(slot, target, send, own=False):
        return pltpu.make_async_remote_copy(
            src_ref=x_ref if own else o_ref.at[slot],
            dst_ref=o_ref.at[slot],
            send_sem=send,
            recv_sem=recv.at[slot],
            device_id=(grp, target),
            device_id_type=MESH,
        )

    def up(s):
        return copy(index(z - s, y, c), index(z + 1, y, c), s_up.at[s], s == 0)

    def down(s):
        return copy(index(z + s, y, c), index(z - 1, y, c), s_down.at[s], s == 0)

    def across(zz, own=False):
        return copy(index(zz, y, c), index(z, 1 - y, c), s_y.at[zz], own)

    def over(zz, yy, own=False):
        return copy(index(zz, yy, c), index(z, y, 1 - c), s_c.at[zz * 2 + yy], own)

    def pass_on(zz):
        over(zz, y).wait_recv()

    own = pltpu.make_async_copy(x_ref, o_ref.at[me], own_sem)
    own.start()
    for s in range(zs):
        below, above = z - s >= 0, z + s < zs
        if s:
            pl.when(below)(lambda: pass_on(z - s))
        if s < zs - 1:
            pl.when(below & (z + 1 < zs))(lambda: up(s).start())
        if s:
            pl.when(above)(lambda: pass_on(z + s))
        if s < zs - 1:
            pl.when(above & (z >= 1))(lambda: down(s).start())
        if s == 0:
            across(z, True).start()
            over(z, y, True).start()
        else:

            def forward(zz):
                across(zz).start()
                over(zz, y).start()

            pl.when(below)(lambda: forward(z - s))
            pl.when(above)(lambda: forward(z + s))
    reach = [0] + [d * s for s in range(1, zs) for d in (-1, 1)]

    def relay(zz):
        over(zz, 1 - y).wait_recv()
        over(zz, 1 - y).start()

    for d in reach:
        zz = z + d
        pl.when((zz >= 0) & (zz < zs))(lambda: relay(zz))
    for zz in range(zs):
        for yy in range(2):
            copy(index(zz, yy, 1 - c), index(z, y, 1 - c), s_c.at[0]).wait_recv()
    own.wait()
    for s in range(zs - 1):
        pl.when((z - s >= 0) & (z + 1 < zs))(lambda: up(s).wait_send())
        pl.when((z + s < zs) & (z >= 1))(lambda: down(s).wait_send())
    for zz in range(zs):
        across(zz).wait_send()
        for yy in range(2):
            over(zz, yy).wait_send()


def gather(n, x):
    zs = n // 4
    dma = pltpu.SemaphoreType.DMA
    return pl.pallas_call(
        functools.partial(gather_kernel, n),
        out_shape=jax.ShapeDtypeStruct((n,) + x.shape, x.dtype),
        in_specs=[pl.BlockSpec(memory_space=pl.ANY)],
        out_specs=pl.BlockSpec(memory_space=pl.ANY),
        scratch_shapes=[dma, dma((zs,)), dma((zs,)), dma((zs,)), dma((2 * zs,)), dma((n,))],
        compiler_params=pltpu.CompilerParams(
            collective_id=0, has_side_effects=True, vmem_limit_bytes=LIMIT
        ),
        name="gather_coeffs",
    )(x)


def exchange_kernel(
    tile_hbm,
    c_hbm,
    slot_hbm,
    col_hbm,
    count_hbm,
    rows_hbm,
    owner_hbm,
    o_ref,
    tile_ref,
    c_ref,
    slot_ref,
    col_ref,
    count_ref,
    rows_ref,
    owner_ref,
    acc,
    half,
    total,
    packed,
    in_sem,
    out_sem,
):
    aux, _, size, _ = tile_ref.shape
    slots = rows_ref.shape[1]
    groups, rows, width = o_ref.shape
    pairs = (
        (slot_hbm, slot_ref),
        (col_hbm, col_ref),
        (count_hbm, count_ref),
        (rows_hbm, rows_ref),
        (owner_hbm, owner_ref),
        (c_hbm, c_ref),
        (tile_hbm, tile_ref),
    )
    loads = [pltpu.make_async_copy(src, dst, in_sem.at[k]) for k, (src, dst) in enumerate(pairs)]
    for load in loads:
        load.start()
    total[...] = jnp.zeros_like(total)
    acc[...] = jnp.zeros_like(acc)
    for load in loads:
        load.wait()
    for p in range(aux):
        if p:
            acc[...] = jnp.zeros_like(acc)

        def tile_step(t, carry):
            col = pl.ds(pl.multiple_of(col_ref[p, t] * size, size), size)
            dst = pl.ds(pl.multiple_of(slot_ref[p, t] * size, size), size)
            acc[:, dst] += lax.dot_general(
                c_ref[:, col],
                tile_ref[p, t],
                (((1,), (1,)), ((), ())),
                preferred_element_type=jnp.float32,
            )
            return carry

        lax.fori_loop(0, count_ref[p], tile_step, 0)
        half[...] = acc[...].astype(half.dtype)
        for r in range(slots):
            left = half[:, r * size : (r + 1) * size].T
            gram = jnp.dot(left, half[...], preferred_element_type=jnp.float32)
            row = pl.ds(pl.multiple_of(rows_ref[p, r] * size, size), size)
            for s in range(slots):
                column = pl.ds(pl.multiple_of(rows_ref[p, s] * size, size), size)
                total[row, column] += gram[:, s * size : (s + 1) * size]
    if width < total.shape[1]:
        low = lax.broadcasted_iota(jnp.int32, (rows, size), 1) < rows

        def pick(row, group, upper):
            block = total[row, pl.ds(pl.multiple_of(group // 2 * size, size), size)]
            swap = group % 2 == (0 if upper else 1)
            return jnp.where(swap, pltpu.roll(block, rows, 1), block)

        def store(j):
            return pltpu.make_async_copy(packed.at[j], o_ref.at[j], out_sem.at[j])

        def pack(j, carry):
            row = pl.ds(pl.multiple_of(owner_ref[j] * rows, rows), rows)
            for e in range(width // size):
                even = pick(row, owner_ref[lax.rem(j + 2 * e, groups)], False)
                odd = pick(row, owner_ref[lax.rem(j + 2 * e + 1, groups)], True)
                packed[j, :, e * size : (e + 1) * size] = jnp.where(low, even, odd)
            store(j).start()
            return carry

        lax.fori_loop(0, groups, pack, 0)
        for j in range(groups):
            store(j).wait()
        return
    stores = []
    for j in range(groups):
        src = pl.ds(pl.multiple_of(owner_ref[j] * rows, rows), rows)
        stores.append(pltpu.make_async_copy(total.at[src], o_ref.at[j], out_sem.at[j]))
        stores[-1].start()
    for store in stores:
        store.wait()


def exchange(n, width, tiles, coeffs, slot, column, count, rows, owner):
    aux, _, size, _ = tiles.shape
    occupied, region = coeffs.shape
    slots = rows.shape[1]
    anywhere = pl.BlockSpec(memory_space=pl.ANY)
    return pl.pallas_call(
        exchange_kernel,
        out_shape=jax.ShapeDtypeStruct((n, region // n, width), jnp.float32),
        in_specs=[anywhere] * 7,
        out_specs=anywhere,
        scratch_shapes=[
            pltpu.VMEM(tiles.shape, tiles.dtype),
            pltpu.VMEM(coeffs.shape, coeffs.dtype),
            pltpu.SMEM(slot.shape, slot.dtype),
            pltpu.SMEM(column.shape, column.dtype),
            pltpu.SMEM(count.shape, count.dtype),
            pltpu.SMEM(rows.shape, rows.dtype),
            pltpu.SMEM(owner.shape, owner.dtype),
            pltpu.VMEM((occupied, slots * size), jnp.float32),
            pltpu.VMEM((occupied, slots * size), jnp.bfloat16),
            pltpu.VMEM((region, region), jnp.float32),
            pltpu.VMEM((n, region // n, width), jnp.float32),
            pltpu.SemaphoreType.DMA((7,)),
            pltpu.SemaphoreType.DMA((n,)),
        ],
        compiler_params=pltpu.CompilerParams(vmem_limit_bytes=LIMIT),
        name="partial_exchange",
    )(tiles, coeffs, slot, column, count, rows, owner)


def scatter_kernel(
    n,
    factor,
    pos_ref,
    x_ref,
    o_ref,
    acc,
    in1,
    in2,
    in3,
    flip,
    stage,
    load_sem,
    s1,
    r1,
    s2,
    r2,
    s3,
    r3,
    s4,
    r4,
):
    zs = n // 4
    me, z, y, c = place(n)
    grp = lax.axis_index("grp")
    rows, width = acc.shape[1:]
    mirrored = n - width // rows
    if mirrored:
        greet_all(n, me)
    else:
        greet(n, z, y, c)
    planes = [(z + k) % zs for k in [zs // 2 + (k + 1) // 2 * (1 - 2 * (k % 2)) for k in range(zs - 1)]]
    planes.append(z)

    def core_copy(zz, yy):
        k = zz * 2 + yy
        return pltpu.make_async_remote_copy(
            src_ref=x_ref.at[index(zz, yy, 1 - c)],
            dst_ref=in1.at[k],
            send_sem=s1.at[k],
            recv_sem=r1.at[k],
            device_id=(grp, index(z, y, 1 - c)),
            device_id_type=MESH,
        )

    def load(zz, yy):
        k = zz * 2 + yy
        return pltpu.make_async_copy(x_ref.at[index(zz, yy, c)], acc.at[k], load_sem.at[k])

    def y_copy(zz):
        return pltpu.make_async_remote_copy(
            src_ref=acc.at[zz * 2 + 1 - y],
            dst_ref=in2.at[zz],
            send_sem=s2.at[zz],
            recv_sem=r2.at[zz],
            device_id=(grp, index(z, 1 - y, c)),
            device_id_type=MESH,
        )

    def z_copy(zz, slot):
        return pltpu.make_async_remote_copy(
            src_ref=acc.at[zz * 2 + y],
            dst_ref=in3.at[slot],
            send_sem=s3.at[zz],
            recv_sem=r3.at[slot],
            device_id=(grp, index(zz, y, c)),
            device_id_type=MESH,
        )

    order = [(zz, yy) for yy in (1 - y, y) for zz in planes]
    for zz, yy in order:
        core_copy(zz, yy).start()
        load(zz, yy).start()
    for zz in planes:
        k = zz * 2 + 1 - y
        load(zz, 1 - y).wait()
        core_copy(zz, 1 - y).wait_recv()
        acc[k] = acc[k] + in1[k]
        y_copy(zz).start()
    for zz in planes[:-1]:
        k = zz * 2 + y
        load(zz, y).wait()
        core_copy(zz, y).wait_recv()
        y_copy(zz).wait_recv()
        acc[k] = acc[k] + in1[k] + in2[zz]
        z_copy(zz, z).start()
    k = z * 2 + y
    load(z, y).wait()
    core_copy(z, y).wait_recv()
    y_copy(z).wait_recv()
    acc[k] = acc[k] + in1[k] + in2[z]
    for zz in planes[:-1]:
        z_copy(zz, zz).wait_recv()
        acc[k] = acc[k] + in3[zz]
    if mirrored:
        size = 2 * rows
        low = lax.broadcasted_iota(jnp.int32, (rows, size), 1) < rows

        def mirror(d):
            return pltpu.make_async_remote_copy(
                src_ref=flip.at[d],
                dst_ref=stage.at[n - d],
                send_sem=s4.at[d],
                recv_sem=r4.at[d],
                device_id=(grp, (me + d) % n),
                device_id_type=MESH,
            )

        for e in range(width // size):
            pair = acc[k, :, e * size : (e + 1) * size] * factor
            turned = pltpu.roll(pair, rows, 1)
            for d, block in (
                (2 * e, jnp.where(low, pair, turned)),
                (2 * e + 1, jnp.where(low, turned, pair)),
            ):
                stage[d] = block
                if 1 <= d <= mirrored:
                    flip[d] = jnp.concatenate([block, block], axis=0).T[:rows]
                    mirror(d).start()
        for d in range(1, mirrored + 1):
            mirror(d).wait_recv()
        for q in range(n // 2):
            even = stage[lax.rem(pos_ref[2 * q] - me + n, n)]
            odd = stage[lax.rem(pos_ref[2 * q + 1] - me + n, n)]
            o_ref[:, q * size : (q + 1) * size] = jnp.where(low, even, odd)
        for d in range(1, mirrored + 1):
            mirror(d).wait_send()
    else:
        o_ref[...] = acc[k] * factor
    for zz, yy in order:
        core_copy(zz, yy).wait_send()
    for zz in planes:
        y_copy(zz).wait_send()
    for zz in planes[:-1]:
        z_copy(zz, z).wait_send()


def scatter(n, factor, region, pos, x):
    zs = n // 4
    block = x.shape[1:]
    rows = block[0]
    dma = pltpu.SemaphoreType.DMA
    return pl.pallas_call(
        functools.partial(scatter_kernel, n, factor),
        out_shape=jax.ShapeDtypeStruct((rows, region), x.dtype),
        in_specs=[pl.BlockSpec(memory_space=pltpu.SMEM), pl.BlockSpec(memory_space=pl.ANY)],
        out_specs=pl.BlockSpec(memory_space=pltpu.VMEM),
        scratch_shapes=[
            pltpu.VMEM((n // 2,) + block, x.dtype),
            pltpu.VMEM((n // 2,) + block, x.dtype),
            pltpu.VMEM((zs,) + block, x.dtype),
            pltpu.VMEM((zs,) + block, x.dtype),
            pltpu.VMEM((n, rows, 2 * rows), x.dtype),
            pltpu.VMEM((n, rows, 2 * rows), x.dtype),
            dma((n // 2,)),
            dma((n // 2,)),
            dma((n // 2,)),
            dma((zs,)),
            dma((zs,)),
            dma((zs,)),
            dma((zs,)),
            dma((n,)),
            dma((n,)),
        ],
        compiler_params=pltpu.CompilerParams(
            collective_id=1, has_side_effects=True, vmem_limit_bytes=LIMIT
        ),
        name="scatter_exchange",
    )(pos, x)


def local(tile_blocks, occupied_coeffs, tile_slot, tile_column, tile_count, row_blocks, owner_map):
    n = lax.axis_size("occ")
    aux_local = tile_blocks.shape[0]
    occupied = occupied_coeffs.shape[0] * n
    region = occupied_coeffs.shape[1]
    factor = 1.0 / math.sqrt(row_blocks.shape[0] * occupied)
    coeffs = gather(n, occupied_coeffs).reshape(occupied, region)
    own_rows = lax.dynamic_slice_in_dim(row_blocks, lax.axis_index("occ") * aux_local, aux_local, 0)
    rows = region // n
    halved = 2 * rows == tile_blocks.shape[2] and n % 4 == 0 and n >= 8
    width = (n // 2 + 2) * rows if halved else region
    order = jnp.arange(n, dtype=jnp.int32)
    pos = jnp.sum(jnp.where(owner_map[None, :] == order[:, None], order[None, :], 0), axis=1)
    partial = exchange(
        n, width, tile_blocks, coeffs, tile_slot, tile_column, tile_count, own_rows, owner_map
    )
    return scatter(n, factor, region, pos, partial)


def solution(mesh):
    in_specs = (
        P(("grp", "occ"), None, None, None),
        P(("grp", "occ"), None),
        P(("grp", "occ"), None),
        P(("grp", "occ"), None),
        P(("grp", "occ")),
        P("grp", None),
        P("grp"),
    )
    out_specs = P(("grp", "occ"), None)
    return jax.shard_map(local, mesh=mesh, in_specs=in_specs, out_specs=out_specs, check_vma=False)
```

```python
import functools
import math

import jax
import jax.numpy as jnp
from jax import lax
from jax.experimental import pallas as pl
from jax.experimental.pallas import tpu as pltpu
from jax.sharding import PartitionSpec as P

MESH = pl.DeviceIdType.MESH
LIMIT = 60 * 1024 * 1024


def place(n):
    me = lax.axis_index("occ")
    return me, me // 4, (me // 2) % 2, me % 2


def index(z, y, c):
    return z * 4 + y * 2 + c


def greet_all(n, me):
    grp = lax.axis_index("grp")
    barrier = pltpu.get_barrier_semaphore()
    for k in range(1, n):
        pl.semaphore_signal(
            barrier, inc=1, device_id=(grp, (me + k) % n), device_id_type=MESH
        )
    pl.semaphore_wait(barrier, n - 1)


def greet(n, z, y, c):
    zs = n // 4
    grp = lax.axis_index("grp")
    others = [index((z + k) % zs, y, c) for k in range(1, zs)]
    others += [index(z, 1 - y, c), index(z, y, 1 - c)]
    barrier = pltpu.get_barrier_semaphore()
    for other in others:
        pl.semaphore_signal(barrier, inc=1, device_id=(grp, other), device_id_type=MESH)
    pl.semaphore_wait(barrier, len(others))


def gather_kernel(n, x_ref, o_ref, own_sem, s_up, s_down, s_y, s_c, recv):
    zs = n // 4
    me, z, y, c = place(n)
    grp = lax.axis_index("grp")
    greet(n, z, y, c)

    def copy(slot, target, send, own=False):
        return pltpu.make_async_remote_copy(
            src_ref=x_ref if own else o_ref.at[slot],
            dst_ref=o_ref.at[slot],
            send_sem=send,
            recv_sem=recv.at[slot],
            device_id=(grp, target),
            device_id_type=MESH,
        )

    def up(s):
        return copy(index(z - s, y, c), index(z + 1, y, c), s_up.at[s], s == 0)

    def down(s):
        return copy(index(z + s, y, c), index(z - 1, y, c), s_down.at[s], s == 0)

    def across(zz, own=False):
        return copy(index(zz, y, c), index(z, 1 - y, c), s_y.at[zz], own)

    def over(zz, yy, own=False):
        return copy(index(zz, yy, c), index(z, y, 1 - c), s_c.at[zz * 2 + yy], own)

    def pass_on(zz):
        over(zz, y).wait_recv()

    own = pltpu.make_async_copy(x_ref, o_ref.at[me], own_sem)
    own.start()
    for s in range(zs):
        below, above = z - s >= 0, z + s < zs
        if s:
            pl.when(below)(lambda: pass_on(z - s))
        if s < zs - 1:
            pl.when(below & (z + 1 < zs))(lambda: up(s).start())
        if s:
            pl.when(above)(lambda: pass_on(z + s))
        if s < zs - 1:
            pl.when(above & (z >= 1))(lambda: down(s).start())
        if s == 0:
            across(z, True).start()
            over(z, y, True).start()
        else:

            def forward(zz):
                across(zz).start()
                over(zz, y).start()

            pl.when(below)(lambda: forward(z - s))
            pl.when(above)(lambda: forward(z + s))
    reach = [0] + [d * s for s in range(1, zs) for d in (-1, 1)]

    def relay(zz):
        over(zz, 1 - y).wait_recv()
        over(zz, 1 - y).start()

    for d in reach:
        zz = z + d
        pl.when((zz >= 0) & (zz < zs))(lambda: relay(zz))
    for zz in range(zs):
        for yy in range(2):
            copy(index(zz, yy, 1 - c), index(z, y, 1 - c), s_c.at[0]).wait_recv()
    own.wait()
    for s in range(zs - 1):
        pl.when((z - s >= 0) & (z + 1 < zs))(lambda: up(s).wait_send())
        pl.when((z + s < zs) & (z >= 1))(lambda: down(s).wait_send())
    for zz in range(zs):
        across(zz).wait_send()
        for yy in range(2):
            over(zz, yy).wait_send()


def gather(n, x):
    zs = n // 4
    dma = pltpu.SemaphoreType.DMA
    return pl.pallas_call(
        functools.partial(gather_kernel, n),
        out_shape=jax.ShapeDtypeStruct((n,) + x.shape, x.dtype),
        in_specs=[pl.BlockSpec(memory_space=pl.ANY)],
        out_specs=pl.BlockSpec(memory_space=pl.ANY),
        scratch_shapes=[dma, dma((zs,)), dma((zs,)), dma((zs,)), dma((2 * zs,)), dma((n,))],
        compiler_params=pltpu.CompilerParams(
            collective_id=0, has_side_effects=True, vmem_limit_bytes=LIMIT
        ),
        name="gather_coeffs",
    )(x)


def exchange_kernel(
    tile_hbm,
    c_hbm,
    slot_hbm,
    col_hbm,
    count_hbm,
    rows_hbm,
    owner_hbm,
    o_ref,
    tile_ref,
    c_ref,
    slot_ref,
    col_ref,
    count_ref,
    rows_ref,
    owner_ref,
    acc,
    half,
    total,
    packed,
    in_sem,
    out_sem,
):
    aux, _, size, _ = tile_ref.shape
    slots = rows_ref.shape[1]
    groups, rows, width = o_ref.shape
    pairs = (
        (slot_hbm, slot_ref),
        (col_hbm, col_ref),
        (count_hbm, count_ref),
        (rows_hbm, rows_ref),
        (owner_hbm, owner_ref),
        (c_hbm, c_ref),
        (tile_hbm, tile_ref),
    )
    loads = [pltpu.make_async_copy(src, dst, in_sem.at[k]) for k, (src, dst) in enumerate(pairs)]
    for load in loads:
        load.start()
    total[...] = jnp.zeros_like(total)
    acc[...] = jnp.zeros_like(acc)
    for load in loads:
        load.wait()
    for p in range(aux):
        if p:
            acc[...] = jnp.zeros_like(acc)

        def product(t, tile):
            col = pl.ds(pl.multiple_of(col_ref[p, t] * size, size), size)
            return lax.dot_general(
                c_ref[:, col], tile, (((1,), (1,)), ((), ())), preferred_element_type=jnp.float32
            )

        def add(t, value):
            dst = pl.ds(pl.multiple_of(slot_ref[p, t] * size, size), size)
            acc[:, dst] += value

        def tile_step(k, carry):
            t = 2 * k
            live = t + 1 < count_ref[p]
            second = tile_ref[p, t + 1]
            a = product(t, tile_ref[p, t])
            b = product(t + 1, jnp.where(live, second, jnp.zeros_like(second)))
            add(t, a)
            add(t + 1, b)
            return carry

        lax.fori_loop(0, (count_ref[p] + 1) // 2, tile_step, 0)
        half[...] = acc[...].astype(half.dtype)
        for r in range(slots):
            left = half[:, r * size : (r + 1) * size].T
            gram = jnp.dot(left, half[...], preferred_element_type=jnp.float32)
            row = pl.ds(pl.multiple_of(rows_ref[p, r] * size, size), size)
            for s in range(slots):
                column = pl.ds(pl.multiple_of(rows_ref[p, s] * size, size), size)
                total[row, column] += gram[:, s * size : (s + 1) * size]
    if width < total.shape[1]:
        low = lax.broadcasted_iota(jnp.int32, (rows, size), 1) < rows

        def pick(row, group, upper):
            block = total[row, pl.ds(pl.multiple_of(group // 2 * size, size), size)]
            swap = group % 2 == (0 if upper else 1)
            return jnp.where(swap, pltpu.roll(block, rows, 1), block)

        def store(j):
            return pltpu.make_async_copy(packed.at[j], o_ref.at[j], out_sem.at[j])

        def pack(j, carry):
            row = pl.ds(pl.multiple_of(owner_ref[j] * rows, rows), rows)
            for e in range(width // size):
                even = pick(row, owner_ref[lax.rem(j + 2 * e, groups)], False)
                odd = pick(row, owner_ref[lax.rem(j + 2 * e + 1, groups)], True)
                packed[j, :, e * size : (e + 1) * size] = jnp.where(low, even, odd)
            store(j).start()
            return carry

        lax.fori_loop(0, groups, pack, 0)
        for j in range(groups):
            store(j).wait()
        return
    stores = []
    for j in range(groups):
        src = pl.ds(pl.multiple_of(owner_ref[j] * rows, rows), rows)
        stores.append(pltpu.make_async_copy(total.at[src], o_ref.at[j], out_sem.at[j]))
        stores[-1].start()
    for store in stores:
        store.wait()


def exchange(n, width, tiles, coeffs, slot, column, count, rows, owner):
    aux, _, size, _ = tiles.shape
    occupied, region = coeffs.shape
    slots = rows.shape[1]
    anywhere = pl.BlockSpec(memory_space=pl.ANY)
    return pl.pallas_call(
        exchange_kernel,
        out_shape=jax.ShapeDtypeStruct((n, region // n, width), jnp.float32),
        in_specs=[anywhere] * 7,
        out_specs=anywhere,
        scratch_shapes=[
            pltpu.VMEM(tiles.shape, tiles.dtype),
            pltpu.VMEM(coeffs.shape, coeffs.dtype),
            pltpu.SMEM(slot.shape, slot.dtype),
            pltpu.SMEM(column.shape, column.dtype),
            pltpu.SMEM(count.shape, count.dtype),
            pltpu.SMEM(rows.shape, rows.dtype),
            pltpu.SMEM(owner.shape, owner.dtype),
            pltpu.VMEM((occupied, slots * size), jnp.float32),
            pltpu.VMEM((occupied, slots * size), jnp.bfloat16),
            pltpu.VMEM((region, region), jnp.float32),
            pltpu.VMEM((n, region // n, width), jnp.float32),
            pltpu.SemaphoreType.DMA((7,)),
            pltpu.SemaphoreType.DMA((n,)),
        ],
        compiler_params=pltpu.CompilerParams(vmem_limit_bytes=LIMIT),
        name="partial_exchange",
    )(tiles, coeffs, slot, column, count, rows, owner)


def scatter_kernel(
    n,
    factor,
    pos_ref,
    x_ref,
    o_ref,
    acc,
    in1,
    in2,
    in3,
    flip,
    stage,
    load_sem,
    s1,
    r1,
    s2,
    r2,
    s3,
    r3,
    s4,
    r4,
):
    zs = n // 4
    me, z, y, c = place(n)
    grp = lax.axis_index("grp")
    rows, width = acc.shape[1:]
    mirrored = n - width // rows
    if mirrored:
        greet_all(n, me)
    else:
        greet(n, z, y, c)
    planes = [(z + k) % zs for k in [zs // 2 + (k + 1) // 2 * (1 - 2 * (k % 2)) for k in range(zs - 1)]]
    planes.append(z)

    def core_copy(zz, yy):
        k = zz * 2 + yy
        return pltpu.make_async_remote_copy(
            src_ref=x_ref.at[index(zz, yy, 1 - c)],
            dst_ref=in1.at[k],
            send_sem=s1.at[k],
            recv_sem=r1.at[k],
            device_id=(grp, index(z, y, 1 - c)),
            device_id_type=MESH,
        )

    def load(zz, yy):
        k = zz * 2 + yy
        return pltpu.make_async_copy(x_ref.at[index(zz, yy, c)], acc.at[k], load_sem.at[k])

    def y_copy(zz):
        return pltpu.make_async_remote_copy(
            src_ref=acc.at[zz * 2 + 1 - y],
            dst_ref=in2.at[zz],
            send_sem=s2.at[zz],
            recv_sem=r2.at[zz],
            device_id=(grp, index(z, 1 - y, c)),
            device_id_type=MESH,
        )

    def z_copy(zz, slot):
        return pltpu.make_async_remote_copy(
            src_ref=acc.at[zz * 2 + y],
            dst_ref=in3.at[slot],
            send_sem=s3.at[zz],
            recv_sem=r3.at[slot],
            device_id=(grp, index(zz, y, c)),
            device_id_type=MESH,
        )

    order = [(zz, yy) for yy in (1 - y, y) for zz in planes]
    ahead = 3
    for zz, yy in order[:ahead]:
        core_copy(zz, yy).start()
    for zz, yy in order:
        load(zz, yy).start()

    def core_arrived(nth):
        core_copy(*order[nth]).wait_recv()
        if nth + ahead < len(order):
            core_copy(*order[nth + ahead]).start()

    for nth, zz in enumerate(planes):
        k = zz * 2 + 1 - y
        load(zz, 1 - y).wait()
        core_arrived(nth)
        acc[k] = acc[k] + in1[k]
        y_copy(zz).start()
    for nth, zz in enumerate(planes[:-1]):
        k = zz * 2 + y
        load(zz, y).wait()
        core_arrived(zs + nth)
        y_copy(zz).wait_recv()
        acc[k] = acc[k] + in1[k] + in2[zz]
        z_copy(zz, z).start()
    k = z * 2 + y
    load(z, y).wait()
    core_arrived(2 * zs - 1)
    y_copy(z).wait_recv()
    acc[k] = acc[k] + in1[k] + in2[z]
    for zz in planes[:-1]:
        z_copy(zz, zz).wait_recv()
        acc[k] = acc[k] + in3[zz]
    if mirrored:
        size = 2 * rows
        low = lax.broadcasted_iota(jnp.int32, (rows, size), 1) < rows

        def mirror(d):
            return pltpu.make_async_remote_copy(
                src_ref=flip.at[d],
                dst_ref=stage.at[n - d],
                send_sem=s4.at[d],
                recv_sem=r4.at[d],
                device_id=(grp, (me + d) % n),
                device_id_type=MESH,
            )

        for e in range(width // size):
            pair = acc[k, :, e * size : (e + 1) * size] * factor
            turned = pltpu.roll(pair, rows, 1)
            for d, block in (
                (2 * e, jnp.where(low, pair, turned)),
                (2 * e + 1, jnp.where(low, turned, pair)),
            ):
                stage[d] = block
                if 1 <= d <= mirrored:
                    flip[d] = jnp.concatenate([block, block], axis=0).T[:rows]
                    mirror(d).start()
        for d in range(1, mirrored + 1):
            mirror(d).wait_recv()
        for q in range(n // 2):
            even = stage[lax.rem(pos_ref[2 * q] - me + n, n)]
            odd = stage[lax.rem(pos_ref[2 * q + 1] - me + n, n)]
            o_ref[:, q * size : (q + 1) * size] = jnp.where(low, even, odd)
        for d in range(1, mirrored + 1):
            mirror(d).wait_send()
    else:
        o_ref[...] = acc[k] * factor
    for zz, yy in order:
        core_copy(zz, yy).wait_send()
    for zz in planes:
        y_copy(zz).wait_send()
    for zz in planes[:-1]:
        z_copy(zz, z).wait_send()


def scatter(n, factor, region, pos, x):
    zs = n // 4
    block = x.shape[1:]
    rows = block[0]
    dma = pltpu.SemaphoreType.DMA
    return pl.pallas_call(
        functools.partial(scatter_kernel, n, factor),
        out_shape=jax.ShapeDtypeStruct((rows, region), x.dtype),
        in_specs=[pl.BlockSpec(memory_space=pltpu.SMEM), pl.BlockSpec(memory_space=pl.ANY)],
        out_specs=pl.BlockSpec(memory_space=pltpu.VMEM),
        scratch_shapes=[
            pltpu.VMEM((n // 2,) + block, x.dtype),
            pltpu.VMEM((n // 2,) + block, x.dtype),
            pltpu.VMEM((zs,) + block, x.dtype),
            pltpu.VMEM((zs,) + block, x.dtype),
            pltpu.VMEM((n, rows, 2 * rows), x.dtype),
            pltpu.VMEM((n, rows, 2 * rows), x.dtype),
            dma((n // 2,)),
            dma((n // 2,)),
            dma((n // 2,)),
            dma((zs,)),
            dma((zs,)),
            dma((zs,)),
            dma((zs,)),
            dma((n,)),
            dma((n,)),
        ],
        compiler_params=pltpu.CompilerParams(
            collective_id=1, has_side_effects=True, vmem_limit_bytes=LIMIT
        ),
        name="scatter_exchange",
    )(pos, x)


def local(tile_blocks, occupied_coeffs, tile_slot, tile_column, tile_count, row_blocks, owner_map):
    n = lax.axis_size("occ")
    aux_local = tile_blocks.shape[0]
    occupied = occupied_coeffs.shape[0] * n
    region = occupied_coeffs.shape[1]
    factor = 1.0 / math.sqrt(row_blocks.shape[0] * occupied)
    coeffs = gather(n, occupied_coeffs).reshape(occupied, region)
    own_rows = lax.dynamic_slice_in_dim(row_blocks, lax.axis_index("occ") * aux_local, aux_local, 0)
    rows = region // n
    halved = 2 * rows == tile_blocks.shape[2] and n % 4 == 0 and n >= 8
    width = (n // 2 + 2) * rows if halved else region
    order = jnp.arange(n, dtype=jnp.int32)
    pos = jnp.sum(jnp.where(owner_map[None, :] == order[:, None], order[None, :], 0), axis=1)
    partial = exchange(
        n, width, tile_blocks, coeffs, tile_slot, tile_column, tile_count, own_rows, owner_map
    )
    return scatter(n, factor, region, pos, partial)


def solution(mesh):
    in_specs = (
        P(("grp", "occ"), None, None, None),
        P(("grp", "occ"), None),
        P(("grp", "occ"), None),
        P(("grp", "occ"), None),
        P(("grp", "occ")),
        P("grp", None),
        P("grp"),
    )
    out_specs = P(("grp", "occ"), None)
    return jax.shard_map(local, mesh=mesh, in_specs=in_specs, out_specs=out_specs, check_vma=False)
```

```python
import functools
import math

import jax
import jax.numpy as jnp
from jax import lax
from jax.experimental import pallas as pl
from jax.experimental.pallas import tpu as pltpu
from jax.sharding import PartitionSpec as P

MESH = pl.DeviceIdType.MESH
LIMIT = 60 * 1024 * 1024


def place(n):
    me = lax.axis_index("occ")
    return me, me // 4, (me // 2) % 2, me % 2


def index(z, y, c):
    return z * 4 + y * 2 + c


def greet_all(n, me):
    grp = lax.axis_index("grp")
    barrier = pltpu.get_barrier_semaphore()
    for k in range(1, n):
        pl.semaphore_signal(
            barrier, inc=1, device_id=(grp, (me + k) % n), device_id_type=MESH
        )
    pl.semaphore_wait(barrier, n - 1)


def greet(n, z, y, c):
    zs = n // 4
    grp = lax.axis_index("grp")
    others = [index((z + k) % zs, y, c) for k in range(1, zs)]
    others += [index(z, 1 - y, c), index(z, y, 1 - c)]
    barrier = pltpu.get_barrier_semaphore()
    for other in others:
        pl.semaphore_signal(barrier, inc=1, device_id=(grp, other), device_id_type=MESH)
    pl.semaphore_wait(barrier, len(others))


def gather_kernel(n, x_ref, o_ref, own_sem, sz, sy, sc, recv):
    zs = n // 4
    me, z, y, c = place(n)
    grp = lax.axis_index("grp")
    greet(n, z, y, c)

    def copy(src, slot, target, send):
        return pltpu.make_async_remote_copy(
            src_ref=src,
            dst_ref=o_ref.at[slot],
            send_sem=send,
            recv_sem=recv.at[slot],
            device_id=(grp, target),
            device_id_type=MESH,
        )

    def arrived(slot):
        copy(o_ref.at[slot], slot, index(z, y, 1 - c), sz.at[0]).wait_recv()

    sent = []

    def send(src, slot, target, sem):
        d = copy(src, slot, target, sem)
        d.start()
        sent.append(d)

    own = pltpu.make_async_copy(x_ref, o_ref.at[me], own_sem)
    own.start()
    for k in range(1, zs):
        send(x_ref, me, index((z + k) % zs, y, c), sz.at[k])
    send(x_ref, me, index(z, 1 - y, c), sy.at[0])
    send(x_ref, me, index(z, y, 1 - c), sc.at[0])
    for k in range(1, zs):
        slot = index((z + zs - k) % zs, y, c)
        arrived(slot)
        send(o_ref.at[slot], slot, index(z, 1 - y, c), sy.at[k])
        send(o_ref.at[slot], slot, index(z, y, 1 - c), sc.at[k])
    for k in range(zs):
        slot = index((z + zs - k) % zs, 1 - y, c)
        arrived(slot)
        send(o_ref.at[slot], slot, index(z, y, 1 - c), sc.at[zs + k])
    for k in range(zs):
        arrived(index((z + zs - k) % zs, y, 1 - c))
        arrived(index((z + zs - k) % zs, 1 - y, 1 - c))
    own.wait()
    for d in sent:
        d.wait_send()


def gather(n, x):
    zs = n // 4
    return pl.pallas_call(
        functools.partial(gather_kernel, n),
        out_shape=jax.ShapeDtypeStruct((n,) + x.shape, x.dtype),
        in_specs=[pl.BlockSpec(memory_space=pl.ANY)],
        out_specs=pl.BlockSpec(memory_space=pl.ANY),
        scratch_shapes=[
            pltpu.SemaphoreType.DMA,
            pltpu.SemaphoreType.DMA((zs,)),
            pltpu.SemaphoreType.DMA((zs,)),
            pltpu.SemaphoreType.DMA((2 * zs,)),
            pltpu.SemaphoreType.DMA((n,)),
        ],
        compiler_params=pltpu.CompilerParams(
            collective_id=0, has_side_effects=True, vmem_limit_bytes=LIMIT
        ),
        name="gather_coeffs",
    )(x)


def exchange_kernel(
    tile_hbm,
    c_hbm,
    slot_hbm,
    col_hbm,
    count_hbm,
    rows_hbm,
    owner_hbm,
    o_ref,
    tile_ref,
    c_ref,
    slot_ref,
    col_ref,
    count_ref,
    rows_ref,
    owner_ref,
    acc,
    half,
    total,
    packed,
    in_sem,
    out_sem,
):
    aux, _, size, _ = tile_ref.shape
    slots = rows_ref.shape[1]
    groups, rows, width = o_ref.shape
    pairs = (
        (slot_hbm, slot_ref),
        (col_hbm, col_ref),
        (count_hbm, count_ref),
        (rows_hbm, rows_ref),
        (owner_hbm, owner_ref),
        (c_hbm, c_ref),
        (tile_hbm, tile_ref),
    )
    loads = [pltpu.make_async_copy(src, dst, in_sem.at[k]) for k, (src, dst) in enumerate(pairs)]
    for load in loads:
        load.start()
    total[...] = jnp.zeros_like(total)
    acc[...] = jnp.zeros_like(acc)
    for load in loads:
        load.wait()
    for p in range(aux):
        if p:
            acc[...] = jnp.zeros_like(acc)

        def product(t, tile):
            col = pl.ds(pl.multiple_of(col_ref[p, t] * size, size), size)
            return lax.dot_general(
                c_ref[:, col], tile, (((1,), (1,)), ((), ())), preferred_element_type=jnp.float32
            )

        def add(t, value):
            dst = pl.ds(pl.multiple_of(slot_ref[p, t] * size, size), size)
            acc[:, dst] += value

        def tile_step(k, carry):
            t = 2 * k
            live = t + 1 < count_ref[p]
            second = tile_ref[p, t + 1]
            a = product(t, tile_ref[p, t])
            b = product(t + 1, jnp.where(live, second, jnp.zeros_like(second)))
            add(t, a)
            add(t + 1, b)
            return carry

        lax.fori_loop(0, (count_ref[p] + 1) // 2, tile_step, 0)
        half[...] = acc[...].astype(half.dtype)
        for r in range(slots):
            left = half[:, r * size : (r + 1) * size].T
            gram = jnp.dot(left, half[...], preferred_element_type=jnp.float32)
            row = pl.ds(pl.multiple_of(rows_ref[p, r] * size, size), size)
            for s in range(slots):
                column = pl.ds(pl.multiple_of(rows_ref[p, s] * size, size), size)
                total[row, column] += gram[:, s * size : (s + 1) * size]
    if width < total.shape[1]:
        low = lax.broadcasted_iota(jnp.int32, (rows, size), 1) < rows

        def pick(row, group, upper):
            block = total[row, pl.ds(pl.multiple_of(group // 2 * size, size), size)]
            swap = group % 2 == (0 if upper else 1)
            return jnp.where(swap, pltpu.roll(block, rows, 1), block)

        def store(j):
            return pltpu.make_async_copy(packed.at[j], o_ref.at[j], out_sem.at[j])

        def pack(j, carry):
            row = pl.ds(pl.multiple_of(owner_ref[j] * rows, rows), rows)
            for e in range(width // size):
                even = pick(row, owner_ref[lax.rem(j + 2 * e, groups)], False)
                odd = pick(row, owner_ref[lax.rem(j + 2 * e + 1, groups)], True)
                packed[j, :, e * size : (e + 1) * size] = jnp.where(low, even, odd)
            store(j).start()
            return carry

        lax.fori_loop(0, groups, pack, 0)
        for j in range(groups):
            store(j).wait()
        return
    stores = []
    for j in range(groups):
        src = pl.ds(pl.multiple_of(owner_ref[j] * rows, rows), rows)
        stores.append(pltpu.make_async_copy(total.at[src], o_ref.at[j], out_sem.at[j]))
        stores[-1].start()
    for store in stores:
        store.wait()


def exchange(n, width, tiles, coeffs, slot, column, count, rows, owner):
    aux, _, size, _ = tiles.shape
    occupied, region = coeffs.shape
    slots = rows.shape[1]
    anywhere = pl.BlockSpec(memory_space=pl.ANY)
    return pl.pallas_call(
        exchange_kernel,
        out_shape=jax.ShapeDtypeStruct((n, region // n, width), jnp.float32),
        in_specs=[anywhere] * 7,
        out_specs=anywhere,
        scratch_shapes=[
            pltpu.VMEM(tiles.shape, tiles.dtype),
            pltpu.VMEM(coeffs.shape, coeffs.dtype),
            pltpu.SMEM(slot.shape, slot.dtype),
            pltpu.SMEM(column.shape, column.dtype),
            pltpu.SMEM(count.shape, count.dtype),
            pltpu.SMEM(rows.shape, rows.dtype),
            pltpu.SMEM(owner.shape, owner.dtype),
            pltpu.VMEM((occupied, slots * size), jnp.float32),
            pltpu.VMEM((occupied, slots * size), jnp.bfloat16),
            pltpu.VMEM((region, region), jnp.float32),
            pltpu.VMEM((n, region // n, width), jnp.float32),
            pltpu.SemaphoreType.DMA((7,)),
            pltpu.SemaphoreType.DMA((n,)),
        ],
        compiler_params=pltpu.CompilerParams(vmem_limit_bytes=LIMIT),
        name="partial_exchange",
    )(tiles, coeffs, slot, column, count, rows, owner)


def scatter_kernel(
    n,
    factor,
    pos_ref,
    x_ref,
    o_ref,
    acc,
    in1,
    in2,
    in3,
    flip,
    stage,
    load_sem,
    s1,
    r1,
    s2,
    r2,
    s3,
    r3,
    s4,
    r4,
):
    zs = n // 4
    me, z, y, c = place(n)
    grp = lax.axis_index("grp")
    rows, width = acc.shape[1:]
    mirrored = n - width // rows
    if mirrored:
        greet_all(n, me)
    else:
        greet(n, z, y, c)
    planes = [(z + k) % zs for k in [zs // 2 + (k + 1) // 2 * (1 - 2 * (k % 2)) for k in range(zs - 1)]]
    planes.append(z)

    def core_copy(zz, yy):
        k = zz * 2 + yy
        return pltpu.make_async_remote_copy(
            src_ref=x_ref.at[index(zz, yy, 1 - c)],
            dst_ref=in1.at[k],
            send_sem=s1.at[k],
            recv_sem=r1.at[k],
            device_id=(grp, index(z, y, 1 - c)),
            device_id_type=MESH,
        )

    def load(zz, yy):
        k = zz * 2 + yy
        return pltpu.make_async_copy(x_ref.at[index(zz, yy, c)], acc.at[k], load_sem.at[k])

    def y_copy(zz):
        return pltpu.make_async_remote_copy(
            src_ref=acc.at[zz * 2 + 1 - y],
            dst_ref=in2.at[zz],
            send_sem=s2.at[zz],
            recv_sem=r2.at[zz],
            device_id=(grp, index(z, 1 - y, c)),
            device_id_type=MESH,
        )

    def z_copy(zz, slot):
        return pltpu.make_async_remote_copy(
            src_ref=acc.at[zz * 2 + y],
            dst_ref=in3.at[slot],
            send_sem=s3.at[zz],
            recv_sem=r3.at[slot],
            device_id=(grp, index(zz, y, c)),
            device_id_type=MESH,
        )

    order = [(zz, yy) for yy in (1 - y, y) for zz in planes]
    ahead = 3
    for zz, yy in order[:ahead]:
        core_copy(zz, yy).start()
    for zz, yy in order:
        load(zz, yy).start()

    def core_arrived(nth):
        core_copy(*order[nth]).wait_recv()
        if nth + ahead < len(order):
            core_copy(*order[nth + ahead]).start()

    for nth, zz in enumerate(planes):
        k = zz * 2 + 1 - y
        load(zz, 1 - y).wait()
        core_arrived(nth)
        acc[k] = acc[k] + in1[k]
        y_copy(zz).start()
    for nth, zz in enumerate(planes[:-1]):
        k = zz * 2 + y
        load(zz, y).wait()
        core_arrived(zs + nth)
        y_copy(zz).wait_recv()
        acc[k] = acc[k] + in1[k] + in2[zz]
        z_copy(zz, z).start()
    k = z * 2 + y
    load(z, y).wait()
    core_arrived(2 * zs - 1)
    y_copy(z).wait_recv()
    acc[k] = acc[k] + in1[k] + in2[z]
    for zz in planes[:-1]:
        z_copy(zz, zz).wait_recv()
        acc[k] = acc[k] + in3[zz]
    if mirrored:
        size = 2 * rows
        low = lax.broadcasted_iota(jnp.int32, (rows, size), 1) < rows

        def mirror(d):
            return pltpu.make_async_remote_copy(
                src_ref=flip.at[d],
                dst_ref=stage.at[n - d],
                send_sem=s4.at[d],
                recv_sem=r4.at[d],
                device_id=(grp, (me + d) % n),
                device_id_type=MESH,
            )

        for e in range(width // size):
            pair = acc[k, :, e * size : (e + 1) * size] * factor
            turned = pltpu.roll(pair, rows, 1)
            for d, block in (
                (2 * e, jnp.where(low, pair, turned)),
                (2 * e + 1, jnp.where(low, turned, pair)),
            ):
                stage[d] = block
                if 1 <= d <= mirrored:
                    flip[d] = jnp.concatenate([block, block], axis=0).T[:rows]
                    mirror(d).start()
        for d in range(1, mirrored + 1):
            mirror(d).wait_recv()
        for q in range(n // 2):
            even = stage[lax.rem(pos_ref[2 * q] - me + n, n)]
            odd = stage[lax.rem(pos_ref[2 * q + 1] - me + n, n)]
            o_ref[:, q * size : (q + 1) * size] = jnp.where(low, even, odd)
        for d in range(1, mirrored + 1):
            mirror(d).wait_send()
    else:
        o_ref[...] = acc[k] * factor
    for zz, yy in order:
        core_copy(zz, yy).wait_send()
    for zz in planes:
        y_copy(zz).wait_send()
    for zz in planes[:-1]:
        z_copy(zz, z).wait_send()


def scatter(n, factor, region, pos, x):
    zs = n // 4
    block = x.shape[1:]
    rows = block[0]
    dma = pltpu.SemaphoreType.DMA
    return pl.pallas_call(
        functools.partial(scatter_kernel, n, factor),
        out_shape=jax.ShapeDtypeStruct((rows, region), x.dtype),
        in_specs=[pl.BlockSpec(memory_space=pltpu.SMEM), pl.BlockSpec(memory_space=pl.ANY)],
        out_specs=pl.BlockSpec(memory_space=pltpu.VMEM),
        scratch_shapes=[
            pltpu.VMEM((n // 2,) + block, x.dtype),
            pltpu.VMEM((n // 2,) + block, x.dtype),
            pltpu.VMEM((zs,) + block, x.dtype),
            pltpu.VMEM((zs,) + block, x.dtype),
            pltpu.VMEM((n, rows, 2 * rows), x.dtype),
            pltpu.VMEM((n, rows, 2 * rows), x.dtype),
            dma((n // 2,)),
            dma((n // 2,)),
            dma((n // 2,)),
            dma((zs,)),
            dma((zs,)),
            dma((zs,)),
            dma((zs,)),
            dma((n,)),
            dma((n,)),
        ],
        compiler_params=pltpu.CompilerParams(
            collective_id=1, has_side_effects=True, vmem_limit_bytes=LIMIT
        ),
        name="scatter_exchange",
    )(pos, x)


def local(tile_blocks, occupied_coeffs, tile_slot, tile_column, tile_count, row_blocks, owner_map):
    n = lax.axis_size("occ")
    aux_local = tile_blocks.shape[0]
    occupied = occupied_coeffs.shape[0] * n
    region = occupied_coeffs.shape[1]
    factor = 1.0 / math.sqrt(row_blocks.shape[0] * occupied)
    coeffs = gather(n, occupied_coeffs).reshape(occupied, region)
    own_rows = lax.dynamic_slice_in_dim(row_blocks, lax.axis_index("occ") * aux_local, aux_local, 0)
    rows = region // n
    halved = 2 * rows == tile_blocks.shape[2] and n % 4 == 0 and n >= 8
    width = (n // 2 + 2) * rows if halved else region
    order = jnp.arange(n, dtype=jnp.int32)
    pos = jnp.sum(jnp.where(owner_map[None, :] == order[:, None], order[None, :], 0), axis=1)
    partial = exchange(
        n, width, tile_blocks, coeffs, tile_slot, tile_column, tile_count, own_rows, owner_map
    )
    return scatter(n, factor, region, pos, partial)


def solution(mesh):
    in_specs = (
        P(("grp", "occ"), None, None, None),
        P(("grp", "occ"), None),
        P(("grp", "occ"), None),
        P(("grp", "occ"), None),
        P(("grp", "occ")),
        P("grp", None),
        P("grp"),
    )
    out_specs = P(("grp", "occ"), None)
    return jax.shard_map(local, mesh=mesh, in_specs=in_specs, out_specs=out_specs, check_vma=False)
```
